512 devices in a mesh: elem: 64 (over z, x), param: 8 (over y, core).
Axes of the slice: x: 4, y: 4, z: 16, core: 2. Of those that a mesh axis runs over, the one named last changes fastest.
Arguments:
- coords: bfloat16 [32, 300], P('param'), may hold values from -6 to 6
- basis_rows: bfloat16 [3, 300, 65536], P(None, None, 'elem'), may hold values from -0.375 to 0.375
- connectivity: int32 [65536, 8], P(('elem', 'param')), may hold values from 0 to 1279, as said below
- modulus: float32 [65536], P(('elem', 'param')), may hold values from 0.5 to 15
- stiffness: float32 [24, 24], replicated, may hold values from -1.25 to 1.25
Outputs:
- training: bfloat16 [32, 300, 65536], P(None, None, ('elem', 'param'))
- target: float32 [32, 300], replicated
The draws below stay inside these ranges and needn't reach their ends.
Inputs may be any that keep to these rules, and one draw needn't show every extreme that they name: `connectivity`: A number c of 1024 or more names node c - 1024 of the next node block; the last block's next block is the first. An element's eight corner numbers lie among min(8, 256) consecutive numbers; where these lie in the block is not tied to the element's position.
All inputs are finite; a program needn't handle non-finite values.
Results may differ from the reference program's by a relative error of at most 0.0072.
Values may be sent and summed in bfloat16 or wider, within the bound.
No kernel may reach another device: no remote copies, remote signals or barrier semaphores. Data moves between devices by JAX's collectives and lax.ppermute only.
A program may use at most 64 MiB of HBM per device.

```python
import math
import jax
import jax.numpy as jnp
from jax import lax

MODES = 300
SNAP = 32
NODE_BLK = 1024
GHOST = 256
NODES = 65536
ELEMS = 65536
N_ELEM = 64


def draw_modulus(key, part):
    position = jnp.arange(ELEMS, dtype=jnp.float32)
    rising = 1.0 + 2.0 * position / max(ELEMS - 1, 1)
    factor = jnp.exp(jax.random.uniform(key, (ELEMS,), jnp.float32, math.log(0.5), math.log(5.0)))
    return (rising * factor).astype(jnp.float32)


def draw_connectivity(key, part):
    window = min(8, GHOST)
    top_base = NODE_BLK + GHOST - window
    local_pos = jnp.arange(ELEMS, dtype=jnp.int32) % NODE_BLK
    random_base = jax.random.randint(jax.random.fold_in(key, 37), (ELEMS,), 0, top_base + 1, jnp.int32)
    base_node = jnp.where(local_pos == 0, 0, jnp.where(local_pos == NODE_BLK - 1, top_base, random_base)).astype(jnp.int32)
    scores = jax.random.randint(jax.random.fold_in(key, 31), (ELEMS, 8), 0, 1 << 20, jnp.int32)
    scores = scores * 8 + jnp.arange(8, dtype=jnp.int32)[None, :]
    ordering = jnp.argsort(scores, axis=1).astype(jnp.int32)
    offsets = ordering % window
    return (base_node[:, None] + offsets).astype(jnp.int32)


def draw_basis_rows(key, part):
    spacing = 8
    cells = -(-NODES // spacing)
    coarse = jax.random.normal(jax.random.fold_in(key, 41), (3, MODES, cells + 1), jnp.float32)
    fraction = (jnp.arange(spacing, dtype=jnp.float32) + 0.5) / spacing
    spread_norm = jnp.sqrt((1.0 - fraction) ** 2 + fraction ** 2)
    smooth = (coarse[:, :, :-1, None] * (1.0 - fraction) + coarse[:, :, 1:, None] * fraction) / spread_norm
    smooth = smooth.reshape(3, MODES, cells * spacing)[:, :, :NODES]
    node_pos = (jnp.arange(NODES, dtype=jnp.int32) % NODE_BLK).astype(jnp.float32) / NODE_BLK
    node_levels = jnp.exp(jax.random.uniform(jax.random.fold_in(key, 43), (NODES,), jnp.float32, math.log(0.7), math.log(1.4)))
    rough_part = jax.random.normal(jax.random.fold_in(key, 47), (3, MODES, NODES), jnp.float32)
    amplitude = (0.7 + 0.6 * node_pos) * node_levels
    shared = 0.35 + 0.55 * node_pos
    values = amplitude * (shared * smooth + jnp.sqrt(1.0 - shared * shared) * rough_part) / math.sqrt(MODES)
    return jnp.clip(values, -0.375, 0.375).astype(jnp.bfloat16)


def level_of(rng, extent, shards, smallest, high):
    level, own = 1.0, jax.random.fold_in(rng, 6)
    for axis_at, shards_of in shards:
        steps = jnp.exp(jax.random.uniform(jax.random.fold_in(own, axis_at), (shards_of,), jnp.float32, smallest / len(shards), high / len(shards)))
        level = level * jnp.repeat(steps, extent[axis_at] // shards_of).reshape([-1 if axis == axis_at else 1 for axis in range(len(extent))])
    return level


def scatter_about(key, extent, spread, reach, shards=(), held_as=jnp.bfloat16):
    loudness = level_of(key, extent, shards, -0.22, 0.18) if shards else 1.0
    values = jax.random.normal(key, extent, jnp.float32) * spread * loudness
    return jnp.minimum(jnp.maximum(values, -reach), reach).astype(held_as)


def setup_inputs(seed: int = 0) -> dict:
    key_of = jax.random.split(jax.random.key(seed), 6)
    coords = scatter_about(key_of[0], (SNAP, MODES), 1.0, 6.0, ((0, 8),))
    basis_rows = draw_basis_rows(jax.random.fold_in(key_of[5], 71), 0)
    connectivity = draw_connectivity(jax.random.fold_in(key_of[5], 71), 0)
    modulus = draw_modulus(jax.random.fold_in(key_of[5], 71), 0)
    stiffness = scatter_about(key_of[4], (24, 24), 24 ** -0.5, 1.25, (), jnp.float32)
    return {"coords": coords, "basis_rows": basis_rows, "connectivity": connectivity, "modulus": modulus, "stiffness": stiffness}


def block_columns(displaced, basis_rows, stiffness, corner_ids, mod_block):
    index_table = corner_ids.T
    count = index_table.shape[1]
    snaps = displaced.shape[0]
    corner_disp = displaced[:, :, index_table].reshape(snaps, 24, count).astype(jnp.float32)
    linear = jnp.einsum('kj,sje->ske', stiffness, corner_disp, precision=lax.Precision.HIGHEST)
    forces = (mod_block * (linear + 0.25 * corner_disp * corner_disp * corner_disp)).astype(jnp.bfloat16)
    forces = forces.reshape(snaps, 3, 8, count)
    element_basis = basis_rows[:, :, index_table]
    return jnp.einsum('cmae,scae->sme', element_basis.astype(jnp.float32), forces.astype(jnp.float32), precision=lax.Precision.HIGHEST)

def global_ids(block_id, conn_block):
    following = (block_id + 1) % N_ELEM
    return jnp.where(conn_block < NODE_BLK, block_id * NODE_BLK + conn_block, following * NODE_BLK + conn_block - NODE_BLK).astype(jnp.int32)

def reference(coords, basis_rows, connectivity, modulus, stiffness):
    displaced = jnp.stack([jnp.dot(coords, basis_rows[component], preferred_element_type=jnp.float32) for component in range(3)], axis=1).astype(jnp.bfloat16)
    conn_blocks = connectivity.reshape(N_ELEM, NODE_BLK, 8)
    mod_blocks = modulus.reshape(N_ELEM, NODE_BLK)
    block_ids = jnp.arange(N_ELEM, dtype=jnp.int32)

    def block_stats(inputs):
        block_id, conn_block, mod_block = inputs
        columns = block_columns(displaced, basis_rows, stiffness, global_ids(block_id, conn_block), mod_block)
        return (lax.optimization_barrier(jnp.sum(jnp.sqrt(lax.optimization_barrier(jnp.sum(columns * columns, axis=1))), axis=1)), lax.optimization_barrier(jnp.sum(columns, axis=2)))
    norm_parts, force_parts = lax.map(block_stats, (block_ids, conn_blocks, mod_blocks))
    row_scale = lax.optimization_barrier(jnp.sum(norm_parts, axis=0)) / ELEMS
    target = lax.optimization_barrier(jnp.sum(force_parts, axis=0)) / (row_scale[:, None] * math.sqrt(ELEMS))

    def block_output(inputs):
        block_id, conn_block, mod_block = inputs
        columns = block_columns(displaced, basis_rows, stiffness, global_ids(block_id, conn_block), mod_block)
        return (columns / row_scale[:, None, None]).astype(jnp.bfloat16)
    pieces = lax.map(block_output, (block_ids, conn_blocks, mod_blocks))
    training = jnp.transpose(pieces, (1, 2, 0, 3)).reshape(SNAP, MODES, ELEMS)
    return (training, target)
```

```python
import jax
import jax.numpy as jnp
from jax import lax
from jax.experimental import pallas as pl
from jax.experimental.pallas import tpu as pltpu
from jax.sharding import Mesh
from jax.sharding import PartitionSpec as P

f32, bf16 = jnp.float32, jnp.bfloat16
VMEM = pl.BlockSpec(memory_space=pltpu.VMEM)
PITCH = 40
ELEMS = 65536.0


def iota(shape, dim):
    return lax.broadcasted_iota(jnp.int32, shape, dim)


def dot(a, b):
    return jnp.dot(a, b, preferred_element_type=f32)


def turned(x, by):
    by = by % 4
    return x if by == 0 else pltpu.roll(x, 32 * by, 1)


def pick(pieces, quarter):
    out = pieces[0]
    for q in range(1, 4):
        out = jnp.where(quarter == q, pieces[q], out)
    return out


def in_group(rolled, rows, group, quarter):
    return pick([rolled[(q - group) % 4][rows[q] : rows[q] + 1, :] for q in range(4)], quarter)


def corner_rows(conn, quarter):
    conns = [turned(conn, by) for by in range(4)]
    return [
        jnp.concatenate(
            [in_group(conns, range(4 * h, 4 * h + 4), group, quarter) for h in range(2)], axis=1
        )
        for group in range(4)
    ]


def lane_quarter():
    return iota((1, 128), 1) >> 5


def own_element(lanes):
    return (iota((32, lanes), 1) & 31) == iota((32, lanes), 0)


def local_body(conn_ref, basis_ref, part_ref):
    ids = corner_rows(conn_ref[...], lane_quarter())
    nodes = basis_ref.shape[2]
    for group in range(4):
        hot = (iota((nodes, 256), 0) == ids[group]).astype(f32).astype(bf16)
        for k in range(3):
            part_ref[group, :, k * 256 : (k + 1) * 256] = dot(basis_ref[k], hot).astype(bf16)


def expanded_product(g_ref, x_ref, r_ref, group, pair, diagonal):
    for j in range(24):
        row = jnp.concatenate(
            [x_ref[group, j, 2 * pair + h : 2 * pair + h + 1, :] for h in range(2)], axis=1
        )
        r_ref[j * 32 : (j + 1) * 32, :] = jnp.where(diagonal, row, 0.0).astype(bf16)
    return dot(g_ref[group], r_ref[...])


def stats_body(
    conn_ref, mod_ref, stiff_ref, coords_ref, part_ref, ghost_ref,
    g_ref, x_ref, sums_ref, w_ref, r_ref, d_ref,
):
    quarter = lane_quarter()
    wide, diagonal = own_element(768), own_element(256)
    stiff = stiff_ref[...]
    high = stiff.astype(bf16)
    low = (stiff - high.astype(f32)).astype(bf16)
    spread = ((iota((24, 768), 1) >> 5) == iota((24, 768), 0)).astype(f32).astype(bf16)
    for p, piece in enumerate((high, low)):
        rows = lax.dot_general(piece, spread, (((0,), (0,)), ((), ())), preferred_element_type=f32)
        for j in range(24):
            w_ref[p, j * 32 : (j + 1) * 32, :] = jnp.where(wide, rows[j : j + 1, :], 0.0).astype(bf16)
    ids = corner_rows(conn_ref[...], quarter)
    for group in range(4):
        hot = (iota((256, 256), 0) + 1024 == ids[group]).astype(f32).astype(bf16)
        for k in range(3):
            at = slice(k * 256, (k + 1) * 256)
            ghost = jnp.concatenate([ghost_ref[0, k], ghost_ref[1, k]], axis=1)
            g_ref[group, :, at] = part_ref[group, :, at] + dot(ghost, hot).astype(bf16)
    coords = coords_ref[...]
    for group in range(4):
        d_ref[group * 32 : (group + 1) * 32, :] = dot(coords, g_ref[group]).astype(bf16)
    disp = d_ref[...]
    linear = dot(disp, w_ref[0]) + dot(disp, w_ref[1])
    mods = [turned(mod_ref[...], by) for by in range(4)]
    sums = None
    for group in range(4):
        modulus = jnp.concatenate([in_group(mods, [0] * 4, group, quarter)] * 6, axis=1)
        at = slice(group * 32, (group + 1) * 32)
        d = disp[at, :].astype(f32)
        force = (modulus * (linear[at, :] + 0.25 * d * d * d)).astype(bf16)
        part = lax.dot_general(force, g_ref[group], (((1,), (1,)), ((), ())), preferred_element_type=f32)
        sums = part if sums is None else sums + part
        force = force.astype(f32)
        for c in range(6):
            rolls = [
                [turned(force[8 * t : 8 * t + 8, c * 128 : (c + 1) * 128], by) for by in range(4)]
                for t in range(4)
            ]
            for a in range(4):
                x_ref[group, c * 4 + a] = pick(
                    [rolls[(q - group) % 4][(q - a) % 4] for q in range(4)], quarter
                )
    norms = []
    for pair in range(4):
        total = None
        for group in range(4):
            columns = expanded_product(g_ref, x_ref, r_ref.at[group], group, pair, diagonal)
            norm = jnp.sqrt(jnp.sum(columns * columns, axis=0, keepdims=True))
            norm = jnp.concatenate(
                [turned(norm[:, h * 128 : (h + 1) * 128], -group) for h in range(2)], axis=0
            )
            total = norm if total is None else total + norm
        norms.append(total)
    norms = jnp.concatenate(norms, axis=0)
    norms = jnp.concatenate(
        [jnp.sum(jnp.where(quarter == t, norms, 0.0), axis=1, keepdims=True) for t in range(4)], axis=0
    )
    lane = iota((1, 128), 1)
    last = jnp.concatenate([sums[:, 256:], jnp.zeros((32, 384 - sums.shape[1]), f32)], axis=1)
    last = jnp.where((lane == 44) | (lane == 45), norms, last)
    for half in range(2):
        at = slice(16 * half, 16 * half + 16)
        sums_ref[half, 0:16, :] = sums[at, 0:128]
        sums_ref[half, 16:32, :] = sums[at, 128:256]
        sums_ref[half, 32:40, :] = last[at, :][0:8] + pltpu.roll(last[at, :][8:16], 64, 1)


def columns_body(g_ref, x_ref, columns_ref, r_ref, acc_ref):
    quarter, diagonal = lane_quarter(), own_element(256)
    modes = g_ref.shape[1]
    for pair in range(4):
        for group in range(4):
            acc_ref[group] = expanded_product(g_ref, x_ref, r_ref, group, pair, diagonal)
        for h in range(2):
            lanes = slice(h * 128, (h + 1) * 128)
            for t in range(4):
                out = turned(pick([acc_ref[(q - t) % 4, :, lanes] for q in range(4)], quarter), -t)
                columns_ref[pl.ds(8 * t + 2 * pair + h, modes, stride=PITCH), :] = out


def scaled_body(sums_ref, columns_ref, training_ref, target_ref):
    last = jnp.concatenate(
        [x for h in range(2) for x in (sums_ref[h, 32:40, :], pltpu.roll(sums_ref[h, 32:40, :], 64, 1))],
        axis=0,
    )
    scale = ELEMS / (last[:, 44:45] + last[:, 45:46])
    training_ref[...] = (columns_ref[...] * scale[None]).astype(bf16)

    @pl.when(pl.program_id(0) == 0)
    def _():
        wide = scale * (1.0 / 256.0)
        for h in range(2):
            at = slice(16 * h, 16 * h + 16)
            target_ref[at, 0:128] = sums_ref[h, 0:16, :] * wide[at]
            target_ref[at, 128:256] = sums_ref[h, 16:32, :] * wide[at]
        target_ref[:, 256:300] = (last * wide)[:, 0:44]


def kernel(body, out, ins, scratch=(), flops=0):
    size = sum(x.size * x.dtype.itemsize for x in (*ins, *out))
    return pl.pallas_call(
        body,
        out_shape=out,
        in_specs=[VMEM] * len(ins),
        out_specs=(VMEM,) * len(out),
        scratch_shapes=scratch,
        compiler_params=pltpu.CompilerParams(vmem_limit_bytes=40 * 2**20),
        cost_estimate=pl.CostEstimate(flops=flops, bytes_accessed=size, transcendentals=0),
    )(*ins)


def array(shape, dtype):
    return jax.ShapeDtypeStruct(shape, dtype)


def passed_along(value, axis, by):
    peers = lax.axis_size(axis)
    return lax.ppermute(value, axis, [(i, (i + by) % peers) for i in range(peers)])


def from_each(value, axis):
    peers = lax.axis_size(axis)
    copies = jnp.broadcast_to(value[None], (peers, *value.shape))
    return lax.all_to_all(copies, axis, 0, 0, tiled=True)


def local(coords, basis_rows, connectivity, modulus, stiffness):
    modes = basis_rows.shape[1]
    core = lax.axis_index("core")
    own_half = lax.dynamic_slice_in_dim(basis_rows, core * 128, 128, axis=2)
    ghost_half = passed_along(own_half, ("z", "x"), -1)
    all_coords = from_each(coords, ("y", "core")).reshape(-1, modes)
    corner_ids = connectivity.T
    (part,) = kernel(
        local_body, (array((4, modes, 768), bf16),), (corner_ids, basis_rows), flops=2 * 10**9
    )
    ghost = lax.all_gather(ghost_half, "core")
    rows, forces, sums = kernel(
        stats_body,
        (array((4, modes, 768), bf16), array((4, 24, 8, 128), f32), array((2, 40, 128), f32)),
        (corner_ids, modulus.reshape(1, -1), stiffness, all_coords, part, ghost),
        (pltpu.VMEM((2, 768, 768), bf16), pltpu.VMEM((4, 768, 256), bf16), pltpu.VMEM((128, 768), bf16)),
        flops=3 * 10**9,
    )
    (columns,) = kernel(
        columns_body,
        (array((modes * PITCH, 128), f32),),
        (rows, forces),
        (pltpu.VMEM((768, 256), bf16), pltpu.VMEM((4, modes, 256), f32)),
        flops=2 * 10**9,
    )
    both = lax.all_gather(sums, "core")
    half = lax.dynamic_index_in_dim(both[0] + both[1], core, 0, keepdims=False)
    half = from_each(half, ("x", "y")).sum(axis=0)
    place = lax.broadcasted_iota(jnp.int32, half.shape, 0) >= 32
    lane = lax.broadcasted_iota(jnp.int32, half.shape, 1) & 63
    rounded = lax.reduce_precision(half, 8, 7)
    half = jnp.where(place & (lane == 45), half - rounded, half).astype(bf16)
    half = from_each(half, "z").astype(f32).sum(axis=0)
    totals = lax.all_gather(half, "core")
    step = 60
    training, target = pl.pallas_call(
        scaled_body,
        grid=(modes // step,),
        out_shape=(array((modes, 32, 128), bf16), array((32, modes), f32)),
        in_specs=[
            pl.BlockSpec((2, 40, 128), lambda i: (0, 0, 0)),
            pl.BlockSpec((step, 32, 128), lambda i: (i, 0, 0)),
        ],
        out_specs=(
            pl.BlockSpec((step, 32, 128), lambda i: (i, 0, 0)),
            pl.BlockSpec((32, modes), lambda i: (0, 0)),
        ),
        compiler_params=pltpu.CompilerParams(vmem_limit_bytes=20 * 2**20),
    )(totals, columns.reshape(modes, PITCH, 128))
    return training.transpose(1, 0, 2), target


def solution(mesh):
    split = Mesh(mesh.devices.reshape(16, 4, 4, 2), ("z", "x", "y", "core"))
    elem, param = ("z", "x"), ("y", "core")
    return jax.shard_map(
        local,
        mesh=split,
        in_specs=(P(param, None), P(None, None, elem), P(elem + param, None), P(elem + param), P()),
        out_specs=(P(None, None, elem + param), P()),
        check_vma=False,
    )
```

```python
import jax
import jax.numpy as jnp
from jax import lax
from jax.experimental import pallas as pl
from jax.experimental.pallas import tpu as pltpu
from jax.sharding import Mesh
from jax.sharding import PartitionSpec as P

f32, bf16 = jnp.float32, jnp.bfloat16
VMEM = pl.BlockSpec(memory_space=pltpu.VMEM)
ANY = pl.BlockSpec(memory_space=pl.ANY)
DMA = pltpu.SemaphoreType.DMA
PITCH = 40
ELEMS = 65536.0


def iota(shape, dim):
    return lax.broadcasted_iota(jnp.int32, shape, dim)


def dot(a, b):
    return jnp.dot(a, b, preferred_element_type=f32)


def turned(x, by):
    by = by % 4
    return x if by == 0 else pltpu.roll(x, 32 * by, 1)


def pick(pieces, quarter):
    out = pieces[0]
    for q in range(1, 4):
        out = jnp.where(quarter == q, pieces[q], out)
    return out


def in_group(rolled, rows, group, quarter):
    return pick([rolled[(q - group) % 4][rows[q] : rows[q] + 1, :] for q in range(4)], quarter)


def corner_rows(conn, quarter):
    conns = [turned(conn, by) for by in range(4)]
    return [
        jnp.concatenate(
            [in_group(conns, range(4 * h, 4 * h + 4), group, quarter) for h in range(2)], axis=1
        )
        for group in range(4)
    ]


def lane_quarter():
    return iota((1, 128), 1) >> 5


def own_element(lanes):
    return (iota((32, lanes), 1) & 31) == iota((32, lanes), 0)


def prepare_body(core_ref, coords_ref, basis_ref, half_ref, copies_ref, sem):
    at = pl.ds(pl.multiple_of(core_ref[0] * 128, 128), 128)
    loads = [pltpu.make_async_copy(basis_ref.at[k, :, at], half_ref.at[k], sem.at[k]) for k in range(3)]
    loads += [pltpu.make_async_copy(coords_ref, copies_ref.at[i], sem.at[3 + i]) for i in range(8)]
    for load in loads:
        load.start()
    for load in loads:
        load.wait()


def expanded_product(g_ref, x_ref, r_ref, group, pair, diagonal):
    for j in range(24):
        row = jnp.concatenate(
            [x_ref[group, j, 2 * pair + h : 2 * pair + h + 1, :] for h in range(2)], axis=1
        )
        r_ref[j * 32 : (j + 1) * 32, :] = jnp.where(diagonal, row, 0.0).astype(bf16)
    return dot(g_ref[group], r_ref[...])


def stats_body(
    conn_ref, mod_ref, stiff_ref, coords_ref, basis_ref, ghost_ref,
    columns_ref, sums_ref, g_ref, x_ref, w_ref, r_ref, d_ref, acc_ref, wide_ref,
):
    quarter = lane_quarter()
    wide, diagonal = own_element(768), own_element(256)
    stiff = stiff_ref[...]
    high = stiff.astype(bf16)
    low = (stiff - high.astype(f32)).astype(bf16)
    spread = ((iota((24, 768), 1) >> 5) == iota((24, 768), 0)).astype(f32).astype(bf16)
    for p, piece in enumerate((high, low)):
        rows = lax.dot_general(piece, spread, (((0,), (0,)), ((), ())), preferred_element_type=f32)
        for j in range(24):
            w_ref[p, j * 32 : (j + 1) * 32, :] = jnp.where(wide, rows[j : j + 1, :], 0.0).astype(bf16)
    ids = corner_rows(conn_ref[...], quarter)
    modes, nodes = basis_ref.shape[1:]
    for group in range(4):
        hot = (iota((nodes, 256), 0) == ids[group]).astype(f32).astype(bf16)
        hot_ghost = (iota((256, 256), 0) + nodes == ids[group]).astype(f32).astype(bf16)
        for k in range(3):
            ghost = jnp.concatenate([ghost_ref[0, k], ghost_ref[1, k]], axis=1)
            rows = dot(basis_ref[k], hot) + dot(ghost, hot_ghost)
            g_ref[group, :, k * 256 : (k + 1) * 256] = rows.astype(bf16)
    coords = coords_ref[...]
    for group in range(4):
        d_ref[group * 32 : (group + 1) * 32, :] = dot(coords, g_ref[group]).astype(bf16)
    disp = d_ref[...]
    linear = dot(disp, w_ref[0]) + dot(disp, w_ref[1])
    mods = [turned(mod_ref[...], by) for by in range(4)]
    sums = None
    for group in range(4):
        modulus = jnp.concatenate([in_group(mods, [0] * 4, group, quarter)] * 6, axis=1)
        at = slice(group * 32, (group + 1) * 32)
        d = disp[at, :].astype(f32)
        force = (modulus * (linear[at, :] + 0.25 * d * d * d)).astype(bf16)
        part = lax.dot_general(force, g_ref[group], (((1,), (1,)), ((), ())), preferred_element_type=f32)
        sums = part if sums is None else sums + part
        force = force.astype(f32)
        for c in range(6):
            rolls = [
                [turned(force[8 * t : 8 * t + 8, c * 128 : (c + 1) * 128], by) for by in range(4)]
                for t in range(4)
            ]
            for a in range(4):
                x_ref[group, c * 4 + a] = pick(
                    [rolls[(q - group) % 4][(q - a) % 4] for q in range(4)], quarter
                )
    norms = []
    for pair in range(4):
        total = None
        for group in range(4):
            columns = expanded_product(g_ref, x_ref, r_ref.at[group], group, pair, diagonal)
            acc_ref[group] = columns
            norm = jnp.sqrt(jnp.sum(columns * columns, axis=0, keepdims=True))
            norm = jnp.concatenate(
                [turned(norm[:, h * 128 : (h + 1) * 128], -group) for h in range(2)], axis=0
            )
            total = norm if total is None else total + norm
        norms.append(total)
        for h in range(2):
            lanes = slice(h * 128, (h + 1) * 128)
            for t in range(4):
                out = turned(pick([acc_ref[(q - t) % 4, :, lanes] for q in range(4)], quarter), -t)
                wide_ref[pl.ds(8 * t + 2 * pair + h, modes, stride=PITCH), :] = out
    norms = jnp.concatenate(norms, axis=0)
    norms = jnp.concatenate(
        [jnp.sum(jnp.where(quarter == t, norms, 0.0), axis=1, keepdims=True) for t in range(4)], axis=0
    )
    lane = iota((1, 128), 1)
    last = jnp.concatenate([sums[:, 256:], jnp.zeros((32, 384 - sums.shape[1]), f32)], axis=1)
    rounded = norms.astype(bf16).astype(f32)
    last = jnp.where(lane == 44, rounded, jnp.where(lane == 45, norms - rounded, last))
    for half in range(2):
        at = slice(16 * half, 16 * half + 16)
        packed = jnp.concatenate(
            [
                sums[at, 0:128],
                sums[at, 128:256],
                last[at, :][0:8] + pltpu.roll(last[at, :][8:16], 64, 1),
            ],
            axis=0,
        ).astype(bf16)
        for peer in range(16):
            sums_ref[peer, half] = packed

    def narrow(i, _):
        for j in range(10):
            at = pl.multiple_of((i * 10 + j) * PITCH, 8)
            columns_ref[i * 10 + j] = wide_ref[pl.ds(at, 32), :].astype(bf16)

    lax.fori_loop(0, modes // 10, narrow, None)


def middle_body(arrived_ref, out_ref):
    total = jnp.sum(arrived_ref[...].astype(f32), axis=0)
    row, lane = iota((40, 128), 0), iota((40, 128), 1) & 63
    whole = total + pltpu.roll(total, 127, 1)
    rounded = whole.astype(bf16).astype(f32)
    total = jnp.where((row >= 32) & (lane == 44), rounded, total)
    total = jnp.where((row >= 32) & (lane == 45), pltpu.roll(whole - rounded, 1, 1), total)
    out_ref[...] = jnp.broadcast_to(total.astype(bf16)[None], out_ref.shape)


def scaled_body(sums_ref, columns_ref, training_ref, target_ref, out_ref, sem):
    last = jnp.concatenate(
        [x for h in range(2) for x in (sums_ref[h, 32:40, :], pltpu.roll(sums_ref[h, 32:40, :], 64, 1))],
        axis=0,
    )
    scale = ELEMS / (last[:, 44:45] + last[:, 45:46])
    wide = jnp.broadcast_to(scale, (32, 128))
    steps, step = out_ref.shape[0], out_ref.shape[1]
    stores = []
    for i in range(steps):
        at = slice(i * step, (i + 1) * step)
        out_ref[i] = (columns_ref[at].astype(f32) * wide[None]).astype(bf16)
        stores.append(pltpu.make_async_copy(out_ref.at[i], training_ref.at[at], sem.at[i]))
        stores[-1].start()
    scale = scale * (1.0 / 256.0)
    for h in range(2):
        at = slice(16 * h, 16 * h + 16)
        target_ref[at, 0:128] = sums_ref[h, 0:16, :] * scale[at]
        target_ref[at, 128:256] = sums_ref[h, 16:32, :] * scale[at]
    target_ref[:, 256:300] = (last * scale)[:, 0:44]
    for store in stores:
        store.wait()


def kernel(body, out, ins, scratch=(), flops=0, far=(), scalars=0, room=16):
    size = sum(x.size * x.dtype.itemsize for x in (*ins, *out))
    specs = [ANY if i in far else VMEM for i in range(len(ins) + len(out))]
    specs[:scalars] = [pl.BlockSpec(memory_space=pltpu.SMEM)] * scalars
    return pl.pallas_call(
        body,
        out_shape=out,
        in_specs=specs[: len(ins)],
        out_specs=tuple(specs[len(ins) :]),
        scratch_shapes=scratch,
        compiler_params=pltpu.CompilerParams(vmem_limit_bytes=room * 2**20),
        cost_estimate=pl.CostEstimate(flops=flops, bytes_accessed=size, transcendentals=0),
    )(*ins)


def array(shape, dtype):
    return jax.ShapeDtypeStruct(shape, dtype)


def passed_along(value, axis, by):
    peers = lax.axis_size(axis)
    return lax.ppermute(value, axis, [(i, (i + by) % peers) for i in range(peers)])


def exchanged(copies, axis):
    return lax.all_to_all(copies, axis, 0, 0, tiled=True)


def local(coords, basis_rows, connectivity, modulus, stiffness):
    modes = basis_rows.shape[1]
    core = lax.axis_index("core")
    own_half, copies = kernel(
        prepare_body,
        (array((3, modes, 128), bf16), array((8, *coords.shape), bf16)),
        (core.astype(jnp.int32).reshape(1), coords, basis_rows),
        (DMA((11,)),),
        far=(1, 2),
        scalars=1,
        room=59,
    )
    ghost_half = passed_along(own_half, ("z", "x"), -1)
    all_coords = exchanged(copies, ("y", "core")).reshape(-1, modes)
    ghost = lax.all_gather(ghost_half, "core")
    rows_shape = (4, modes, 768)
    columns, sums = kernel(
        stats_body,
        (array((modes, 32, 128), bf16), array((16, 2, 40, 128), bf16)),
        (connectivity.T, modulus.reshape(1, -1), stiffness, all_coords, basis_rows, ghost),
        (
            pltpu.VMEM((4, modes, 768), bf16),
            pltpu.VMEM((4, 24, 8, 128), f32),
            pltpu.VMEM((2, 768, 768), bf16),
            pltpu.VMEM((4, 768, 256), bf16),
            pltpu.VMEM((128, 768), bf16),
            pltpu.VMEM((4, modes, 256), f32),
            pltpu.VMEM((modes * PITCH, 128), f32),
        ),
        flops=7 * 10**9,
        room=24,
    )
    plane = exchanged(sums.reshape(32, 40, 128), ("x", "y", "core"))
    (plane,) = kernel(middle_body, (array((16, 40, 128), bf16),), (plane,))
    half = exchanged(plane, "z").astype(f32).sum(axis=0)
    totals = lax.all_gather(half, "core")
    step = 60
    training, target = kernel(
        scaled_body,
        (array((modes, 32, 128), bf16), array((32, modes), f32)),
        (totals, columns),
        (pltpu.VMEM((modes // step, step, 32, 128), bf16), DMA((modes // step,))),
        far=(2,),
    )
    return training.transpose(1, 0, 2), target


def solution(mesh):
    split = Mesh(mesh.devices.reshape(16, 4, 4, 2), ("z", "x", "y", "core"))
    elem, param = ("z", "x"), ("y", "core")
    return jax.shard_map(
        local,
        mesh=split,
        in_specs=(P(param, None), P(None, None, elem), P(elem + param, None), P(elem + param), P()),
        out_specs=(P(None, None, elem + param), P()),
        check_vma=False,
    )
```

```python
import jax
import jax.numpy as jnp
from jax import lax
from jax.experimental import pallas as pl
from jax.experimental.pallas import tpu as pltpu
from jax.sharding import Mesh
from jax.sharding import PartitionSpec as P

f32, bf16 = jnp.float32, jnp.bfloat16
VMEM = pl.BlockSpec(memory_space=pltpu.VMEM)
ANY = pl.BlockSpec(memory_space=pl.ANY)
DMA = pltpu.SemaphoreType.DMA
EARLY = 2
PITCH = 40
ELEMS = 65536.0


def iota(shape, dim):
    return lax.broadcasted_iota(jnp.int32, shape, dim)


def dot(a, b):
    return jnp.dot(a, b, preferred_element_type=f32)


def turned(x, by):
    by = by % 4
    return x if by == 0 else pltpu.roll(x, 32 * by, 1)


def pick(pieces, quarter):
    out = pieces[0]
    for q in range(1, 4):
        out = jnp.where(quarter == q, pieces[q], out)
    return out


def in_group(rolled, rows, group, quarter):
    return pick([rolled[(q - group) % 4][rows[q] : rows[q] + 1, :] for q in range(4)], quarter)


def corner_rows(conn, quarter):
    conns = [turned(conn, by) for by in range(4)]
    return [
        jnp.concatenate(
            [in_group(conns, range(4 * h, 4 * h + 4), group, quarter) for h in range(2)], axis=1
        )
        for group in range(4)
    ]


def lane_quarter():
    return iota((1, 128), 1) >> 5


def own_element(lanes):
    return (iota((32, lanes), 1) & 31) == iota((32, lanes), 0)


def prepare_body(core_ref, coords_ref, basis_ref, half_ref, copies_ref, sem):
    at = pl.ds(pl.multiple_of(core_ref[0] * 128, 128), 128)
    loads = [pltpu.make_async_copy(basis_ref.at[k, :, at], half_ref.at[k], sem.at[k]) for k in range(3)]
    loads += [pltpu.make_async_copy(coords_ref, copies_ref.at[i], sem.at[3 + i]) for i in range(8)]
    for load in loads:
        load.start()
    for load in loads:
        load.wait()


def expanded_product(g_ref, x_ref, r_ref, group, pair, diagonal):
    for j in range(24):
        row = jnp.concatenate(
            [x_ref[group, j, 2 * pair + h : 2 * pair + h + 1, :] for h in range(2)], axis=1
        )
        r_ref[j * 32 : (j + 1) * 32, :] = jnp.where(diagonal, row, 0.0).astype(bf16)
    return dot(g_ref[group], r_ref[...])


def local_body(conn_ref, basis_ref, *part_refs):
    ids = corner_rows(conn_ref[...], lane_quarter())
    for group, part_ref in enumerate(part_refs):
        hot = (iota((basis_ref.shape[2], 256), 0) == ids[group]).astype(f32).astype(bf16)
        for k in range(3):
            part_ref[:, k * 256 : (k + 1) * 256] = dot(basis_ref[k], hot).astype(bf16)


def stats_body(
    conn_ref, mod_ref, stiff_ref, coords_ref, basis_ref, ghost_ref, *refs
):
    parts = refs[:EARLY]
    columns_ref, sums_ref, g_ref, x_ref, w_ref, r_ref, d_ref, acc_ref, wide_ref = refs[EARLY:]
    quarter = lane_quarter()
    wide, diagonal = own_element(768), own_element(256)
    stiff = stiff_ref[...]
    high = stiff.astype(bf16)
    low = (stiff - high.astype(f32)).astype(bf16)
    spread = ((iota((24, 768), 1) >> 5) == iota((24, 768), 0)).astype(f32).astype(bf16)
    for p, piece in enumerate((high, low)):
        rows = lax.dot_general(piece, spread, (((0,), (0,)), ((), ())), preferred_element_type=f32)
        for j in range(24):
            w_ref[p, j * 32 : (j + 1) * 32, :] = jnp.where(wide, rows[j : j + 1, :], 0.0).astype(bf16)
    ids = corner_rows(conn_ref[...], quarter)
    modes, nodes = basis_ref.shape[1:]
    for group in range(4):
        if group >= EARLY:
            hot = (iota((nodes, 256), 0) == ids[group]).astype(f32).astype(bf16)
        hot_ghost = (iota((256, 256), 0) + nodes == ids[group]).astype(f32).astype(bf16)
        for k in range(3):
            ghost = jnp.concatenate([ghost_ref[0, k], ghost_ref[1, k]], axis=1)
            at = slice(k * 256, (k + 1) * 256)
            rows = dot(ghost, hot_ghost)
            if group >= EARLY:
                g_ref[group, :, at] = (rows + dot(basis_ref[k], hot)).astype(bf16)
            else:
                g_ref[group, :, at] = rows.astype(bf16) + parts[group][:, at]
    coords = jnp.concatenate([coords_ref[i].astype(f32) for i in range(coords_ref.shape[0])], axis=0)
    coords = coords.astype(bf16)
    for group in range(4):
        d_ref[group * 32 : (group + 1) * 32, :] = dot(coords, g_ref[group]).astype(bf16)
    disp = d_ref[...]
    linear = dot(disp, w_ref[0]) + dot(disp, w_ref[1])
    mods = [turned(mod_ref[...], by) for by in range(4)]
    sums = None
    for group in range(4):
        modulus = jnp.concatenate([in_group(mods, [0] * 4, group, quarter)] * 6, axis=1)
        at = slice(group * 32, (group + 1) * 32)
        d = disp[at, :].astype(f32)
        force = (modulus * (linear[at, :] + 0.25 * d * d * d)).astype(bf16)
        part = lax.dot_general(force, g_ref[group], (((1,), (1,)), ((), ())), preferred_element_type=f32)
        sums = part if sums is None else sums + part
        force = force.astype(f32)
        for c in range(6):
            rolls = [
                [turned(force[8 * t : 8 * t + 8, c * 128 : (c + 1) * 128], by) for by in range(4)]
                for t in range(4)
            ]
            for a in range(4):
                x_ref[group, c * 4 + a] = pick(
                    [rolls[(q - group) % 4][(q - a) % 4] for q in range(4)], quarter
                )
    norms = []
    for pair in range(4):
        total = None
        for group in range(4):
            columns = expanded_product(g_ref, x_ref, r_ref.at[group], group, pair, diagonal)
            acc_ref[group] = columns
            norm = jnp.sqrt(jnp.sum(columns * columns, axis=0, keepdims=True))
            norm = jnp.concatenate(
                [turned(norm[:, h * 128 : (h + 1) * 128], -group) for h in range(2)], axis=0
            )
            total = norm if total is None else total + norm
        norms.append(total)
        for h in range(2):
            lanes = slice(h * 128, (h + 1) * 128)
            for t in range(4):
                out = turned(pick([acc_ref[(q - t) % 4, :, lanes] for q in range(4)], quarter), -t)
                wide_ref[pl.ds(8 * t + 2 * pair + h, modes, stride=PITCH), :] = out
    norms = jnp.concatenate(norms, axis=0)
    norms = jnp.concatenate(
        [jnp.sum(jnp.where(quarter == t, norms, 0.0), axis=1, keepdims=True) for t in range(4)], axis=0
    )
    lane = iota((1, 128), 1)
    last = jnp.concatenate([sums[:, 256:], jnp.zeros((32, 384 - sums.shape[1]), f32)], axis=1)
    rounded = norms.astype(bf16).astype(f32)
    last = jnp.where(lane == 44, rounded, jnp.where(lane == 45, norms - rounded, last))
    for half in range(2):
        at = slice(16 * half, 16 * half + 16)
        packed = jnp.concatenate(
            [
                sums[at, 0:128],
                sums[at, 128:256],
                last[at, :][0:8] + pltpu.roll(last[at, :][8:16], 64, 1),
            ],
            axis=0,
        ).astype(bf16)
        for peer in range(16):
            sums_ref[peer, half] = packed

    def narrow(i, _):
        for j in range(10):
            at = pl.multiple_of((i * 10 + j) * PITCH, 8)
            columns_ref[i * 10 + j] = wide_ref[pl.ds(at, 32), :].astype(bf16)

    lax.fori_loop(0, modes // 10, narrow, None)


def middle_body(arrived_ref, out_ref):
    total = jnp.sum(arrived_ref[...].astype(f32), axis=0)
    row, lane = iota((40, 128), 0), iota((40, 128), 1) & 63
    whole = total + pltpu.roll(total, 127, 1)
    rounded = whole.astype(bf16).astype(f32)
    total = jnp.where((row >= 32) & (lane == 44), rounded, total)
    total = jnp.where((row >= 32) & (lane == 45), pltpu.roll(whole - rounded, 1, 1), total)
    out_ref[...] = jnp.broadcast_to(total.astype(bf16)[None], out_ref.shape)


def scaled_body(sums_ref, columns_ref, training_ref, target_ref, out_ref, sem):
    last = jnp.concatenate(
        [x for h in range(2) for x in (sums_ref[h, 32:40, :], pltpu.roll(sums_ref[h, 32:40, :], 64, 1))],
        axis=0,
    )
    scale = ELEMS / (last[:, 44:45] + last[:, 45:46])
    wide = jnp.broadcast_to(scale, (32, 128))
    steps, step = out_ref.shape[0], out_ref.shape[1]
    stores = []
    for i in range(steps):
        at = slice(i * step, (i + 1) * step)
        out_ref[i] = (columns_ref[at].astype(f32) * wide[None]).astype(bf16)
        stores.append(pltpu.make_async_copy(out_ref.at[i], training_ref.at[at], sem.at[i]))
        stores[-1].start()
    scale = scale * (1.0 / 256.0)
    for h in range(2):
        at = slice(16 * h, 16 * h + 16)
        target_ref[at, 0:128] = sums_ref[h, 0:16, :] * scale[at]
        target_ref[at, 128:256] = sums_ref[h, 16:32, :] * scale[at]
    target_ref[:, 256:300] = (last * scale)[:, 0:44]
    for store in stores:
        store.wait()


def kernel(body, out, ins, scratch=(), flops=0, far=(), scalars=0, room=16):
    size = sum(x.size * x.dtype.itemsize for x in (*ins, *out))
    specs = [ANY if i in far else VMEM for i in range(len(ins) + len(out))]
    specs[:scalars] = [pl.BlockSpec(memory_space=pltpu.SMEM)] * scalars
    return pl.pallas_call(
        body,
        out_shape=out,
        in_specs=specs[: len(ins)],
        out_specs=tuple(specs[len(ins) :]),
        scratch_shapes=scratch,
        compiler_params=pltpu.CompilerParams(vmem_limit_bytes=room * 2**20),
        cost_estimate=pl.CostEstimate(flops=flops, bytes_accessed=size, transcendentals=0),
    )(*ins)


def array(shape, dtype):
    return jax.ShapeDtypeStruct(shape, dtype)


def passed_along(value, axis, by):
    peers = lax.axis_size(axis)
    return lax.ppermute(value, axis, [(i, (i + by) % peers) for i in range(peers)])


def exchanged(copies, axis):
    return lax.all_to_all(copies, axis, 0, 0, tiled=True)


def local(coords, basis_rows, connectivity, modulus, stiffness):
    modes = basis_rows.shape[1]
    core = lax.axis_index("core")
    own_half, copies = kernel(
        prepare_body,
        (array((3, modes, 128), bf16), array((8, *coords.shape), bf16)),
        (core.astype(jnp.int32).reshape(1), coords, basis_rows),
        (DMA((11,)),),
        far=(1, 2),
        scalars=1,
        flops=2 * 10**9,
        room=59,
    )
    ghost_half = passed_along(own_half, ("z", "x"), -1)
    all_coords = exchanged(copies, ("y", "core"))
    corner_ids = connectivity.T
    parts = kernel(
        local_body, (array((modes, 768), bf16),) * EARLY, (corner_ids, basis_rows), flops=2 * 10**9
    )
    ghost = lax.all_gather(ghost_half, "core")
    rows_shape = (4, modes, 768)
    columns, sums = kernel(
        stats_body,
        (array((modes, 32, 128), bf16), array((16, 2, 40, 128), bf16)),
        (corner_ids, modulus.reshape(1, -1), stiffness, all_coords, basis_rows, ghost, *parts),
        (
            pltpu.VMEM((4, modes, 768), bf16),
            pltpu.VMEM((4, 24, 8, 128), f32),
            pltpu.VMEM((2, 768, 768), bf16),
            pltpu.VMEM((4, 768, 256), bf16),
            pltpu.VMEM((128, 768), bf16),
            pltpu.VMEM((4, modes, 256), f32),
            pltpu.VMEM((modes * PITCH, 128), f32),
        ),
        flops=7 * 10**9,
        room=24,
    )
    plane = exchanged(sums.reshape(32, 40, 128), ("x", "y", "core"))
    (plane,) = kernel(middle_body, (array((16, 40, 128), bf16),), (plane,))
    half = exchanged(plane, "z").astype(f32).sum(axis=0)
    totals = lax.all_gather(half, "core")
    step = 30
    training, target = kernel(
        scaled_body,
        (array((modes, 32, 128), bf16), array((32, modes), f32)),
        (totals, columns),
        (pltpu.VMEM((modes // step, step, 32, 128), bf16), DMA((modes // step,))),
        far=(2,),
    )
    return training.transpose(1, 0, 2), target


def solution(mesh):
    split = Mesh(mesh.devices.reshape(16, 4, 4, 2), ("z", "x", "y", "core"))
    elem, param = ("z", "x"), ("y", "core")
    return jax.shard_map(
        local,
        mesh=split,
        in_specs=(P(param, None), P(None, None, elem), P(elem + param, None), P(elem + param), P()),
        out_specs=(P(None, None, elem + param), P()),
        check_vma=False,
    )
```

```python
import jax
import jax.numpy as jnp
from jax import lax
from jax.experimental import pallas as pl
from jax.experimental.pallas import tpu as pltpu
from jax.sharding import Mesh
from jax.sharding import PartitionSpec as P

f32, bf16 = jnp.float32, jnp.bfloat16
VMEM = pl.BlockSpec(memory_space=pltpu.VMEM)
ANY = pl.BlockSpec(memory_space=pl.ANY)
DMA = pltpu.SemaphoreType.DMA
EARLY = 2
PITCH = 40
ELEMS = 65536.0


def iota(shape, dim):
    return lax.broadcasted_iota(jnp.int32, shape, dim)


def dot(a, b):
    return jnp.dot(a, b, preferred_element_type=f32)


def turned(x, by):
    by = by % 4
    return x if by == 0 else pltpu.roll(x, 32 * by, 1)


def pick(pieces, quarter):
    out = pieces[0]
    for q in range(1, 4):
        out = jnp.where(quarter == q, pieces[q], out)
    return out


def in_group(rolled, rows, group, quarter):
    return pick([rolled[(q - group) % 4][rows[q] : rows[q] + 1, :] for q in range(4)], quarter)


def corner_rows(conn, quarter):
    conns = [turned(conn, by) for by in range(4)]
    return [
        jnp.concatenate(
            [in_group(conns, range(4 * h, 4 * h + 4), group, quarter) for h in range(2)], axis=1
        )
        for group in range(4)
    ]


def lane_quarter():
    return iota((1, 128), 1) >> 5


def own_element(lanes):
    return (iota((32, lanes), 1) & 31) == iota((32, lanes), 0)


def copies_body(coords_ref, copies_ref):
    copies_ref[...] = jnp.broadcast_to(coords_ref[...][None], copies_ref.shape)


def expanded_product(g_ref, x_ref, r_ref, group, pair, diagonal):
    for j in range(24):
        row = jnp.concatenate(
            [x_ref[group, j, 2 * pair + h : 2 * pair + h + 1, :] for h in range(2)], axis=1
        )
        r_ref[j * 32 : (j + 1) * 32, :] = jnp.where(diagonal, row, 0.0).astype(bf16)
    return dot(g_ref[group], r_ref[...])


def local_body(conn_ref, basis_ref, *part_refs):
    ids = corner_rows(conn_ref[...], lane_quarter())
    for group, part_ref in enumerate(part_refs):
        hot = (iota((basis_ref.shape[2], 256), 0) == ids[group]).astype(f32).astype(bf16)
        for k in range(3):
            part_ref[:, k * 256 : (k + 1) * 256] = dot(basis_ref[k], hot).astype(bf16)


def stats_body(
    conn_ref, mod_ref, stiff_ref, coords_ref, basis_ref, ghost_ref, *refs
):
    parts = refs[:EARLY]
    columns_ref, sums_ref, g_ref, x_ref, w_ref, r_ref, d_ref, acc_ref, wide_ref = refs[EARLY:]
    quarter = lane_quarter()
    wide, diagonal = own_element(768), own_element(256)
    stiff = stiff_ref[...]
    high = stiff.astype(bf16)
    low = (stiff - high.astype(f32)).astype(bf16)
    spread = ((iota((24, 768), 1) >> 5) == iota((24, 768), 0)).astype(f32).astype(bf16)
    for p, piece in enumerate((high, low)):
        rows = lax.dot_general(piece, spread, (((0,), (0,)), ((), ())), preferred_element_type=f32)
        for j in range(24):
            w_ref[p, j * 32 : (j + 1) * 32, :] = jnp.where(wide, rows[j : j + 1, :], 0.0).astype(bf16)
    ids = corner_rows(conn_ref[...], quarter)
    modes, nodes = basis_ref.shape[1:]
    for group in range(4):
        if group >= EARLY:
            hot = (iota((nodes, 256), 0) == ids[group]).astype(f32).astype(bf16)
        hot_ghost = (iota((256, 256), 0) + nodes == ids[group]).astype(f32).astype(bf16)
        for k in range(3):
            ghost = jnp.concatenate([ghost_ref[0, k], ghost_ref[1, k]], axis=1)
            at = slice(k * 256, (k + 1) * 256)
            rows = dot(ghost, hot_ghost)
            if group >= EARLY:
                g_ref[group, :, at] = (rows + dot(basis_ref[k], hot)).astype(bf16)
            else:
                g_ref[group, :, at] = rows.astype(bf16) + parts[group][:, at]
    coords = jnp.concatenate([coords_ref[i].astype(f32) for i in range(coords_ref.shape[0])], axis=0)
    coords = coords.astype(bf16)
    for group in range(4):
        d_ref[group * 32 : (group + 1) * 32, :] = dot(coords, g_ref[group]).astype(bf16)
    disp = d_ref[...]
    linear = dot(disp, w_ref[0]) + dot(disp, w_ref[1])
    mods = [turned(mod_ref[...], by) for by in range(4)]
    sums = None
    for group in range(4):
        modulus = jnp.concatenate([in_group(mods, [0] * 4, group, quarter)] * 6, axis=1)
        at = slice(group * 32, (group + 1) * 32)
        d = disp[at, :].astype(f32)
        force = (modulus * (linear[at, :] + 0.25 * d * d * d)).astype(bf16)
        part = lax.dot_general(force, g_ref[group], (((1,), (1,)), ((), ())), preferred_element_type=f32)
        sums = part if sums is None else sums + part
        force = force.astype(f32)
        for c in range(6):
            rolls = [
                [turned(force[8 * t : 8 * t + 8, c * 128 : (c + 1) * 128], by) for by in range(4)]
                for t in range(4)
            ]
            for a in range(4):
                x_ref[group, c * 4 + a] = pick(
                    [rolls[(q - group) % 4][(q - a) % 4] for q in range(4)], quarter
                )
    norms = []
    for pair in range(4):
        total = None
        for group in range(4):
            columns = expanded_product(g_ref, x_ref, r_ref.at[group], group, pair, diagonal)
            acc_ref[group] = columns
            norm = jnp.sqrt(jnp.sum(columns * columns, axis=0, keepdims=True))
            norm = jnp.concatenate(
                [turned(norm[:, h * 128 : (h + 1) * 128], -group) for h in range(2)], axis=0
            )
            total = norm if total is None else total + norm
        norms.append(total)
        for h in range(2):
            lanes = slice(h * 128, (h + 1) * 128)
            for t in range(4):
                out = turned(pick([acc_ref[(q - t) % 4, :, lanes] for q in range(4)], quarter), -t)
                wide_ref[pl.ds(8 * t + 2 * pair + h, modes, stride=PITCH), :] = out
    norms = jnp.concatenate(norms, axis=0)
    norms = jnp.concatenate(
        [jnp.sum(jnp.where(quarter == t, norms, 0.0), axis=1, keepdims=True) for t in range(4)], axis=0
    )
    lane = iota((1, 128), 1)
    last = jnp.concatenate([sums[:, 256:], jnp.zeros((32, 384 - sums.shape[1]), f32)], axis=1)
    rounded = norms.astype(bf16).astype(f32)
    last = jnp.where(lane == 44, rounded, jnp.where(lane == 45, norms - rounded, last))
    for half in range(2):
        at = slice(16 * half, 16 * half + 16)
        packed = jnp.concatenate(
            [
                sums[at, 0:128],
                sums[at, 128:256],
                last[at, :][0:8] + pltpu.roll(last[at, :][8:16], 64, 1),
            ],
            axis=0,
        ).astype(bf16)
        for peer in range(16):
            sums_ref[peer, half] = packed

    def narrow(i, _):
        for j in range(10):
            at = pl.multiple_of((i * 10 + j) * PITCH, 8)
            columns_ref[i * 10 + j] = wide_ref[pl.ds(at, 32), :].astype(bf16)

    lax.fori_loop(0, modes // 10, narrow, None)


def middle_body(arrived_ref, out_ref):
    total = jnp.sum(arrived_ref[...].astype(f32), axis=0)
    row, lane = iota((40, 128), 0), iota((40, 128), 1) & 63
    whole = total + pltpu.roll(total, 127, 1)
    rounded = whole.astype(bf16).astype(f32)
    total = jnp.where((row >= 32) & (lane == 44), rounded, total)
    total = jnp.where((row >= 32) & (lane == 45), pltpu.roll(whole - rounded, 1, 1), total)
    out_ref[...] = jnp.broadcast_to(total.astype(bf16)[None], out_ref.shape)


def scaled_body(sums_ref, columns_ref, training_ref, target_ref, out_ref, sem):
    last = jnp.concatenate(
        [x for h in range(2) for x in (sums_ref[h, 32:40, :], pltpu.roll(sums_ref[h, 32:40, :], 64, 1))],
        axis=0,
    )
    scale = ELEMS / (last[:, 44:45] + last[:, 45:46])
    wide = jnp.broadcast_to(scale, (32, 128))
    steps, step = out_ref.shape[0], out_ref.shape[1]
    stores = []
    for i in range(steps):
        at = slice(i * step, (i + 1) * step)
        out_ref[i] = (columns_ref[at].astype(f32) * wide[None]).astype(bf16)
        stores.append(pltpu.make_async_copy(out_ref.at[i], training_ref.at[at], sem.at[i]))
        stores[-1].start()
    scale = scale * (1.0 / 256.0)
    for h in range(2):
        at = slice(16 * h, 16 * h + 16)
        target_ref[at, 0:128] = sums_ref[h, 0:16, :] * scale[at]
        target_ref[at, 128:256] = sums_ref[h, 16:32, :] * scale[at]
    target_ref[:, 256:300] = (last * scale)[:, 0:44]
    for store in stores:
        store.wait()


def kernel(body, out, ins, scratch=(), flops=0, far=(), scalars=0, room=16):
    size = sum(x.size * x.dtype.itemsize for x in (*ins, *out))
    specs = [ANY if i in far else VMEM for i in range(len(ins) + len(out))]
    specs[:scalars] = [pl.BlockSpec(memory_space=pltpu.SMEM)] * scalars
    return pl.pallas_call(
        body,
        out_shape=out,
        in_specs=specs[: len(ins)],
        out_specs=tuple(specs[len(ins) :]),
        scratch_shapes=scratch,
        compiler_params=pltpu.CompilerParams(vmem_limit_bytes=room * 2**20),
        cost_estimate=pl.CostEstimate(flops=flops, bytes_accessed=size, transcendentals=0),
    )(*ins)


def array(shape, dtype):
    return jax.ShapeDtypeStruct(shape, dtype)


def passed_along(value, axis, by):
    peers = lax.axis_size(axis)
    return lax.ppermute(value, axis, [(i, (i + by) % peers) for i in range(peers)])


def exchanged(copies, axis):
    return lax.all_to_all(copies, axis, 0, 0, tiled=True)


def local(coords, basis_rows, connectivity, modulus, stiffness):
    modes = basis_rows.shape[1]
    core = lax.axis_index("core")
    own_half = lax.dynamic_slice_in_dim(basis_rows, core * 128, 128, axis=2)
    ghost_half = passed_along(own_half, ("z", "x"), -1)
    (copies,) = kernel(copies_body, (array((8, *coords.shape), bf16),), (coords,), flops=2 * 10**9)
    all_coords = exchanged(copies, ("y", "core"))
    corner_ids = connectivity.T
    parts = kernel(
        local_body, (array((modes, 768), bf16),) * EARLY, (corner_ids, basis_rows), flops=2 * 10**9
    )
    ghost = lax.all_gather(ghost_half, "core")
    rows_shape = (4, modes, 768)
    columns, sums = kernel(
        stats_body,
        (array((modes, 32, 128), bf16), array((16, 2, 40, 128), bf16)),
        (corner_ids, modulus.reshape(1, -1), stiffness, all_coords, basis_rows, ghost, *parts),
        (
            pltpu.VMEM((4, modes, 768), bf16),
            pltpu.VMEM((4, 24, 8, 128), f32),
            pltpu.VMEM((2, 768, 768), bf16),
            pltpu.VMEM((4, 768, 256), bf16),
            pltpu.VMEM((128, 768), bf16),
            pltpu.VMEM((4, modes, 256), f32),
            pltpu.VMEM((modes * PITCH, 128), f32),
        ),
        flops=7 * 10**9,
        room=24,
    )
    plane = exchanged(sums.reshape(32, 40, 128), ("x", "y", "core"))
    (plane,) = kernel(middle_body, (array((16, 40, 128), bf16),), (plane,))
    half = exchanged(plane, "z").astype(f32).sum(axis=0)
    totals = lax.all_gather(half, "core")
    step = 30
    training, target = kernel(
        scaled_body,
        (array((modes, 32, 128), bf16), array((32, modes), f32)),
        (totals, columns),
        (pltpu.VMEM((modes // step, step, 32, 128), bf16), DMA((modes // step,))),
        far=(2,),
    )
    return training.transpose(1, 0, 2), target


def solution(mesh):
    split = Mesh(mesh.devices.reshape(16, 4, 4, 2), ("z", "x", "y", "core"))
    elem, param = ("z", "x"), ("y", "core")
    return jax.shard_map(
        local,
        mesh=split,
        in_specs=(P(param, None), P(None, None, elem), P(elem + param, None), P(elem + param), P()),
        out_specs=(P(None, None, elem + param), P()),
        check_vma=False,
    )
```

```python
import jax
import jax.numpy as jnp
from jax import lax
from jax.experimental import pallas as pl
from jax.experimental.pallas import tpu as pltpu
from jax.sharding import Mesh
from jax.sharding import PartitionSpec as P

f32, bf16 = jnp.float32, jnp.bfloat16
VMEM = pl.BlockSpec(memory_space=pltpu.VMEM)
ANY = pl.BlockSpec(memory_space=pl.ANY)
DMA = pltpu.SemaphoreType.DMA
EARLY = 2
PITCH = 40
ELEMS = 65536.0


def iota(shape, dim):
    return lax.broadcasted_iota(jnp.int32, shape, dim)


def dot(a, b):
    return jnp.dot(a, b, preferred_element_type=f32)


def turned(x, by):
    by = by % 4
    return x if by == 0 else pltpu.roll(x, 32 * by, 1)


def pick(pieces, quarter):
    out = pieces[0]
    for q in range(1, 4):
        out = jnp.where(quarter == q, pieces[q], out)
    return out


def in_group(rolled, rows, group, quarter):
    return pick([rolled[(q - group) % 4][rows[q] : rows[q] + 1, :] for q in range(4)], quarter)


def corner_rows(conn, quarter):
    conns = [turned(conn, by) for by in range(4)]
    return [
        jnp.concatenate(
            [in_group(conns, range(4 * h, 4 * h + 4), group, quarter) for h in range(2)], axis=1
        )
        for group in range(4)
    ]


def lane_quarter():
    return iota((1, 128), 1) >> 5


def own_element(lanes):
    return (iota((32, lanes), 1) & 31) == iota((32, lanes), 0)


def copies_body(coords_ref, copies_ref, sem):
    copies = [pltpu.make_async_copy(coords_ref, copies_ref.at[i], sem.at[i]) for i in range(8)]
    for copy in copies:
        copy.start()
    for copy in copies:
        copy.wait()


def expanded_product(g_ref, x_ref, r_ref, group, pair, diagonal):
    for j in range(24):
        row = jnp.concatenate(
            [x_ref[group, j, 2 * pair + h : 2 * pair + h + 1, :] for h in range(2)], axis=1
        )
        r_ref[j * 32 : (j + 1) * 32, :] = jnp.where(diagonal, row, 0.0).astype(bf16)
    return dot(g_ref[group], r_ref[...])


def local_body(conn_ref, basis_ref, *part_refs):
    ids = corner_rows(conn_ref[...], lane_quarter())
    for group, part_ref in enumerate(part_refs):
        hot = (iota((basis_ref.shape[2], 256), 0) == ids[group]).astype(f32).astype(bf16)
        for k in range(3):
            part_ref[:, k * 256 : (k + 1) * 256] = dot(basis_ref[k], hot).astype(bf16)


def stats_body(
    conn_ref, mod_ref, stiff_ref, coords_ref, basis_ref, ghost_ref, *refs
):
    parts = refs[:EARLY]
    columns_ref, sums_ref, g_ref, x_ref, w_ref, r_ref, d_ref, acc_ref, wide_ref = refs[EARLY:]
    quarter = lane_quarter()
    wide, diagonal = own_element(768), own_element(256)
    stiff = stiff_ref[...]
    high = stiff.astype(bf16)
    low = (stiff - high.astype(f32)).astype(bf16)
    spread = ((iota((24, 768), 1) >> 5) == iota((24, 768), 0)).astype(f32).astype(bf16)
    for p, piece in enumerate((high, low)):
        rows = lax.dot_general(piece, spread, (((0,), (0,)), ((), ())), preferred_element_type=f32)
        for j in range(24):
            w_ref[p, j * 32 : (j + 1) * 32, :] = jnp.where(wide, rows[j : j + 1, :], 0.0).astype(bf16)
    ids = corner_rows(conn_ref[...], quarter)
    modes, nodes = basis_ref.shape[1:]
    for group in range(4):
        if group >= EARLY:
            hot = (iota((nodes, 256), 0) == ids[group]).astype(f32).astype(bf16)
        hot_ghost = (iota((256, 256), 0) + nodes == ids[group]).astype(f32).astype(bf16)
        for k in range(3):
            ghost = jnp.concatenate([ghost_ref[0, k], ghost_ref[1, k]], axis=1)
            at = slice(k * 256, (k + 1) * 256)
            rows = dot(ghost, hot_ghost)
            if group >= EARLY:
                g_ref[group, :, at] = (rows + dot(basis_ref[k], hot)).astype(bf16)
            else:
                g_ref[group, :, at] = rows.astype(bf16) + parts[group][:, at]
    coords = jnp.concatenate([coords_ref[i].astype(f32) for i in range(coords_ref.shape[0])], axis=0)
    coords = coords.astype(bf16)
    for group in range(4):
        d_ref[group * 32 : (group + 1) * 32, :] = dot(coords, g_ref[group]).astype(bf16)
    disp = d_ref[...]
    linear = dot(disp, w_ref[0]) + dot(disp, w_ref[1])
    mods = [turned(mod_ref[...], by) for by in range(4)]
    sums = None
    for group in range(4):
        modulus = jnp.concatenate([in_group(mods, [0] * 4, group, quarter)] * 6, axis=1)
        at = slice(group * 32, (group + 1) * 32)
        d = disp[at, :].astype(f32)
        force = (modulus * (linear[at, :] + 0.25 * d * d * d)).astype(bf16)
        part = lax.dot_general(force, g_ref[group], (((1,), (1,)), ((), ())), preferred_element_type=f32)
        sums = part if sums is None else sums + part
        force = force.astype(f32)
        for c in range(6):
            rolls = [
                [turned(force[8 * t : 8 * t + 8, c * 128 : (c + 1) * 128], by) for by in range(4)]
                for t in range(4)
            ]
            for a in range(4):
                x_ref[group, c * 4 + a] = pick(
                    [rolls[(q - group) % 4][(q - a) % 4] for q in range(4)], quarter
                )
    norms = []
    for pair in range(4):
        total = None
        for group in range(4):
            columns = expanded_product(g_ref, x_ref, r_ref.at[group], group, pair, diagonal)
            acc_ref[group] = columns
            norm = jnp.sqrt(jnp.sum(columns * columns, axis=0, keepdims=True))
            norm = jnp.concatenate(
                [turned(norm[:, h * 128 : (h + 1) * 128], -group) for h in range(2)], axis=0
            )
            total = norm if total is None else total + norm
        norms.append(total)
        for h in range(2):
            lanes = slice(h * 128, (h + 1) * 128)
            for t in range(4):
                out = turned(pick([acc_ref[(q - t) % 4, :, lanes] for q in range(4)], quarter), -t)
                wide_ref[pl.ds(8 * t + 2 * pair + h, modes, stride=PITCH), :] = out
    norms = jnp.concatenate(norms, axis=0)
    norms = jnp.concatenate(
        [jnp.sum(jnp.where(quarter == t, norms, 0.0), axis=1, keepdims=True) for t in range(4)], axis=0
    )
    lane = iota((1, 128), 1)
    last = jnp.concatenate([sums[:, 256:], jnp.zeros((32, 384 - sums.shape[1]), f32)], axis=1)
    rounded = norms.astype(bf16).astype(f32)
    last = jnp.where(lane == 44, rounded, jnp.where(lane == 45, norms - rounded, last))
    for half in range(2):
        at = slice(16 * half, 16 * half + 16)
        packed = jnp.concatenate(
            [
                sums[at, 0:128],
                sums[at, 128:256],
                last[at, :][0:8] + pltpu.roll(last[at, :][8:16], 64, 1),
            ],
            axis=0,
        ).astype(bf16)
        for peer in range(16):
            sums_ref[peer, half] = packed

    def narrow(i, _):
        for j in range(10):
            at = pl.multiple_of((i * 10 + j) * PITCH, 8)
            columns_ref[i * 10 + j] = wide_ref[pl.ds(at, 32), :].astype(bf16)

    lax.fori_loop(0, modes // 10, narrow, None)


def middle_body(arrived_ref, out_ref):
    total = jnp.sum(arrived_ref[...].astype(f32), axis=0)
    row, lane = iota((40, 128), 0), iota((40, 128), 1) & 63
    whole = total + pltpu.roll(total, 127, 1)
    rounded = whole.astype(bf16).astype(f32)
    total = jnp.where((row >= 32) & (lane == 44), rounded, total)
    total = jnp.where((row >= 32) & (lane == 45), pltpu.roll(whole - rounded, 1, 1), total)
    out_ref[...] = jnp.broadcast_to(total.astype(bf16)[None], out_ref.shape)


def scaled_body(sums_ref, columns_ref, training_ref, target_ref, out_ref, sem):
    last = jnp.concatenate(
        [x for h in range(2) for x in (sums_ref[h, 32:40, :], pltpu.roll(sums_ref[h, 32:40, :], 64, 1))],
        axis=0,
    )
    scale = ELEMS / (last[:, 44:45] + last[:, 45:46])
    wide = jnp.broadcast_to(scale, (32, 128))
    steps, step = out_ref.shape[0], out_ref.shape[1]
    stores = []
    for i in range(steps):
        at = slice(i * step, (i + 1) * step)
        out_ref[i] = (columns_ref[at].astype(f32) * wide[None]).astype(bf16)
        stores.append(pltpu.make_async_copy(out_ref.at[i], training_ref.at[at], sem.at[i]))
        stores[-1].start()
    scale = scale * (1.0 / 256.0)
    for h in range(2):
        at = slice(16 * h, 16 * h + 16)
        target_ref[at, 0:128] = sums_ref[h, 0:16, :] * scale[at]
        target_ref[at, 128:256] = sums_ref[h, 16:32, :] * scale[at]
    target_ref[:, 256:300] = (last * scale)[:, 0:44]
    for store in stores:
        store.wait()


def kernel(body, out, ins, scratch=(), flops=0, far=(), scalars=0, room=16):
    size = sum(x.size * x.dtype.itemsize for x in (*ins, *out))
    specs = [ANY if i in far else VMEM for i in range(len(ins) + len(out))]
    specs[:scalars] = [pl.BlockSpec(memory_space=pltpu.SMEM)] * scalars
    return pl.pallas_call(
        body,
        out_shape=out,
        in_specs=specs[: len(ins)],
        out_specs=tuple(specs[len(ins) :]),
        scratch_shapes=scratch,
        compiler_params=pltpu.CompilerParams(vmem_limit_bytes=room * 2**20),
        cost_estimate=pl.CostEstimate(flops=flops, bytes_accessed=size, transcendentals=0),
    )(*ins)


def array(shape, dtype):
    return jax.ShapeDtypeStruct(shape, dtype)


def passed_along(value, axis, by):
    peers = lax.axis_size(axis)
    return lax.ppermute(value, axis, [(i, (i + by) % peers) for i in range(peers)])


def exchanged(copies, axis):
    return lax.all_to_all(copies, axis, 0, 0, tiled=True)


def local(coords, basis_rows, connectivity, modulus, stiffness):
    modes = basis_rows.shape[1]
    core = lax.axis_index("core")
    own_half = lax.dynamic_slice_in_dim(basis_rows, core * 128, 128, axis=2)
    ghost_half = passed_along(own_half, ("z", "x"), -1)
    (copies,) = kernel(copies_body, (array((8, *coords.shape), bf16),), (coords,), (DMA((8,)),), flops=2 * 10**9, far=(0, 1), room=60)
    all_coords = exchanged(copies, ("y", "core"))
    corner_ids = connectivity.T
    parts = kernel(
        local_body, (array((modes, 768), bf16),) * EARLY, (corner_ids, basis_rows), flops=2 * 10**9
    )
    ghost = lax.all_gather(ghost_half, "core")
    rows_shape = (4, modes, 768)
    columns, sums = kernel(
        stats_body,
        (array((modes, 32, 128), bf16), array((16, 2, 40, 128), bf16)),
        (corner_ids, modulus.reshape(1, -1), stiffness, all_coords, basis_rows, ghost, *parts),
        (
            pltpu.VMEM((4, modes, 768), bf16),
            pltpu.VMEM((4, 24, 8, 128), f32),
            pltpu.VMEM((2, 768, 768), bf16),
            pltpu.VMEM((4, 768, 256), bf16),
            pltpu.VMEM((128, 768), bf16),
            pltpu.VMEM((4, modes, 256), f32),
            pltpu.VMEM((modes * PITCH, 128), f32),
        ),
        flops=7 * 10**9,
        room=24,
    )
    plane = exchanged(sums.reshape(32, 40, 128), ("x", "y", "core"))
    (plane,) = kernel(middle_body, (array((16, 40, 128), bf16),), (plane,))
    half = exchanged(plane, "z").astype(f32).sum(axis=0)
    totals = lax.all_gather(half, "core")
    step = 30
    training, target = kernel(
        scaled_body,
        (array((modes, 32, 128), bf16), array((32, modes), f32)),
        (totals, columns),
        (pltpu.VMEM((modes // step, step, 32, 128), bf16), DMA((modes // step,))),
        far=(2,),
    )
    return training.transpose(1, 0, 2), target


def solution(mesh):
    split = Mesh(mesh.devices.reshape(16, 4, 4, 2), ("z", "x", "y", "core"))
    elem, param = ("z", "x"), ("y", "core")
    return jax.shard_map(
        local,
        mesh=split,
        in_specs=(P(param, None), P(None, None, elem), P(elem + param, None), P(elem + param), P()),
        out_specs=(P(None, None, elem + param), P()),
        check_vma=False,
    )
```
